512 devices in a mesh: seq: 64 (over z_hi, x, y, core), head: 8 (over z_lo).
Axes of the slice: x: 4, y: 4, z: 16 (z_hi: 2, z_lo: 8; z = z_hi * 8 + z_lo), core: 2. Of those that a mesh axis runs over, the one named last changes fastest.
Arguments:
- queries: bfloat16 [32768, 12288], P('seq', 'head'), may hold values from -100 to 100
- latent: bfloat16 [32768, 512], P('seq', 'head'), may hold values from -6 to 6
- key_rope: bfloat16 [32768, 64], P('seq'), may hold values from -6 to 6
- key_up: bfloat16 [512, 8192], P(None, 'head'), may hold values from -0.25 to 0.25
- value_up: bfloat16 [512, 8192], P(None, 'head'), may hold values from -0.25 to 0.25
- block_ids: int32 [128], P('seq'), may hold values from 0 to 127, each once
Outputs:
- attended: bfloat16 [32768, 8192], P('seq', 'head')
The draws below stay inside these ranges and needn't reach their ends.
Inputs may be any that keep to these rules, and one draw needn't show every extreme that they name: `block_ids`: every block number appears once.
All inputs are finite; a program needn't handle non-finite values.
Results may differ from the reference program's by a relative error of at most 0.006.
Values may be sent and summed in bfloat16 or wider, within the bound.
No kernel may reach another device: no remote copies, remote signals or barrier semaphores. Data moves between devices by JAX's collectives and lax.ppermute only.
A program may use at most 64 MiB of HBM per device.

```python
import jax
import jax.numpy as jnp
from jax import lax

LAT = 512
ROPE = 64
NOPE = 128
VAL = 128
TOK_DEV = 512
BLOCK = 256
BLOCKS = 128
TOKENS = 32768
HEADS = 64
N_SEQ = 64


def draw_key_rope(key, part):
    key = jax.random.fold_in(key, 3)
    value = jnp.clip(jax.random.normal(key, (TOKENS, ROPE), jnp.float32), -6.0, 6.0)
    return value.astype(jnp.bfloat16)


def draw_queries(key, part):
    key = jax.random.fold_in(key, 7)
    value = jnp.clip(jax.random.normal(key, (TOKENS, HEADS, NOPE + ROPE), jnp.float32), -6.0, 6.0)
    return value.reshape(TOKENS, HEADS * (NOPE + ROPE)).astype(jnp.bfloat16)


def level_of(rng, dims, shards, low, high):
    def one(axis_at, shards_of):
        heights = jax.random.uniform(jax.random.fold_in(jax.random.fold_in(rng, 6), axis_at), (shards_of,), jnp.float32, low / len(shards), high / len(shards))
        return jnp.repeat(jnp.exp(heights), dims[axis_at] // shards_of).reshape((-1,) + (1,) * (len(dims) - axis_at - 1))

    level = one(*shards[0])
    for cut in shards[1:]:
        level = level * one(*cut)
    return level


def scatter_about(rng, dims, width, bound, shards=(), kind=jnp.bfloat16):
    values = width * jax.random.normal(rng, dims, jnp.float32)
    if shards:
        values = values * level_of(rng, dims, shards, -0.22, 0.18)
    return jnp.clip(values, -bound, bound).astype(kind)


def setup_inputs(seed: int = 0) -> dict:
    seeds = jax.random.split(jax.random.key(seed), 7)
    queries = draw_queries(jax.random.fold_in(seeds[6], 71), 0)
    latent = scatter_about(seeds[1], (TOKENS, LAT), 1.0, 6.0, ((0, 64), (1, 8)))
    key_rope = draw_key_rope(jax.random.fold_in(seeds[6], 71), 0)
    key_up = scatter_about(seeds[3], (LAT, HEADS * NOPE), LAT ** -0.5, 0.25, ((1, 8),))
    value_up = scatter_about(seeds[4], (LAT, HEADS * VAL), LAT ** -0.5, 0.25, ((1, 8),))
    block_ids = jax.random.permutation(seeds[5], BLOCKS).astype(jnp.int32)
    return dict(queries=queries, latent=latent, key_rope=key_rope, key_up=key_up, value_up=value_up, block_ids=block_ids)


def reference(queries, latent, key_rope, key_up, value_up, block_ids):
    key_nope = jnp.dot(latent, key_up, preferred_element_type=jnp.float32).astype(jnp.bfloat16)
    value_all = jnp.dot(latent, value_up, preferred_element_type=jnp.float32).astype(jnp.bfloat16)
    row_ids = jnp.arange(TOKENS, dtype=jnp.int32)
    position = block_ids[row_ids // BLOCK] * BLOCK + row_ids % BLOCK
    score_scale = 1.0 / jnp.sqrt(jnp.float32(NOPE + ROPE))

    def one_group(group):
        first_row = (group * TOK_DEV).astype(jnp.int32)
        prior_row = ((group + N_SEQ - 1) % N_SEQ * TOK_DEV).astype(jnp.int32)

        def rows_of(array):
            return jnp.concatenate([lax.dynamic_slice_in_dim(array, first_row, TOK_DEV, 0), lax.dynamic_slice_in_dim(array, prior_row, TOK_DEV, 0)], axis=0)
        query_rows = lax.dynamic_slice_in_dim(queries, first_row, TOK_DEV, 0).reshape(TOK_DEV, HEADS, NOPE + ROPE)
        key_rows = rows_of(key_nope).reshape(2 * TOK_DEV, HEADS, NOPE)
        rope_rows = rows_of(key_rope)
        value_rows = rows_of(value_all).reshape(2 * TOK_DEV, HEADS, VAL)
        query_pos = lax.dynamic_slice_in_dim(position, first_row, TOK_DEV, 0)
        key_pos = rows_of(position)
        allowed = key_pos[None, :] <= query_pos[:, None]
        score = jnp.einsum('qhd,khd->hqk', query_rows[:, :, :NOPE].astype(jnp.float32), key_rows.astype(jnp.float32))
        score = score + jnp.einsum('qhd,kd->hqk', query_rows[:, :, NOPE:].astype(jnp.float32), rope_rows.astype(jnp.float32))
        score = score * score_scale
        score = jnp.where(allowed[None], score, jnp.float32(-1e+30))
        top = lax.optimization_barrier(jnp.max(score, axis=-1, keepdims=True))
        weight = jnp.where(allowed[None], jnp.exp(score - top), jnp.float32(0.0))
        total = lax.optimization_barrier(jnp.sum(weight, axis=-1))
        weight = weight.astype(jnp.bfloat16)
        summed = jnp.einsum('hqk,khd->qhd', weight.astype(jnp.float32), value_rows.astype(jnp.float32))
        result = summed / jnp.transpose(total)[:, :, None]
        return result.reshape(TOK_DEV, HEADS * VAL).astype(jnp.bfloat16)
    groups = lax.map(one_group, jnp.arange(N_SEQ, dtype=jnp.int32))
    return groups.reshape(TOKENS, HEADS * VAL)
```

```python
import math

import jax
import jax.numpy as jnp
from jax import lax
from jax.experimental import pallas as pl
from jax.experimental.pallas import tpu as pltpu
from jax.sharding import PartitionSpec as P

ROPE = 64
NOPE = 128
VAL = 128
BLOCK = 256
SHARD = 64
ID_ROWS = 16
GAIN = math.log2(math.e) / math.sqrt(NOPE + ROPE)
ORDER = (0, 4, 2, 1, 5, 3, 6, 7)
NEAR = 3
F32 = jnp.float32
BF16 = jnp.bfloat16


def dot(a, b):
    return jnp.dot(a, b, preferred_element_type=F32)


def place(pieces, at, first, lat):
    rows = [(piece, r) for piece in pieces for r in range(0, piece.shape[0], SHARD)]
    other = pl.multiple_of(BLOCK - first, BLOCK)
    for (piece, r), which in zip(rows, ORDER, strict=True):
        to = pl.ds(pl.multiple_of((at ^ which) * SHARD, SHARD), SHARD)
        lat[to, :BLOCK] = piece[r : r + SHARD, pl.ds(first, BLOCK)]
        lat[to, BLOCK:] = piece[r : r + SHARD, pl.ds(other, BLOCK)]


def place_rope(rope_in, first, keys):
    other = pl.multiple_of(BLOCK - first, BLOCK)
    rope = jnp.concatenate([rope_in[:, pl.ds(first, BLOCK)], rope_in[:, pl.ds(other, BLOCK)]], axis=1)
    none = jnp.zeros_like(rope)
    for head in range(keys.shape[0]):
        if head % 2 == 0:
            keys[head, NOPE : NOPE + ROPE, :] = rope
            keys[head, NOPE + ROPE :, :] = none
        else:
            keys[head, :ROPE, :] = none
            keys[head, ROPE + NOPE :, :] = rope


def project(lat, key_up_t, value_up, keys, values):
    features = lat[...]
    for pair in range(keys.shape[0] // 2):
        part = dot(key_up_t[pair * 256 : (pair + 1) * 256, :], features).astype(BF16)
        keys[2 * pair, :NOPE, :] = part[:NOPE]
        keys[2 * pair + 1, ROPE : ROPE + NOPE, :] = part[NOPE:]
    rows = features.T
    for pair in range(keys.shape[0] // 2):
        columns = slice(pair * 256, (pair + 1) * 256)
        values[:, columns] = dot(rows, value_up[:, columns]).astype(BF16)


def own_kernel(ids, queries, a, b, c, d, rope, key_up_t, value_up, acc_out, stat_out, lat, keys, values):
    first = pl.multiple_of(jnp.where(ids[0] < ids[1], 0, BLOCK), BLOCK)
    other = pl.multiple_of(BLOCK - first, BLOCK)
    place((a, b, c, d), lax.axis_index("head"), first, lat)
    place_rope(rope, first, keys)
    project(lat, key_up_t, value_up, keys, values)
    heads = keys.shape[0]
    row = lax.broadcasted_iota(jnp.int32, (BLOCK, BLOCK), 0)
    col = lax.broadcasted_iota(jnp.int32, (BLOCK, BLOCK), 1)
    seen = col <= row
    lane = lax.broadcasted_iota(jnp.int32, (BLOCK, 128), 1)
    stat = [jnp.zeros((BLOCK, 128), F32)] * 2
    ones = jnp.ones((2 * BLOCK, VAL), BF16)
    for head in range(heads):
        base = (head // 2) * 384 + (head % 2) * 128
        columns = slice(head * VAL, (head + 1) * VAL)
        value = jnp.concatenate([values[:, columns], ones], axis=1)
        for part, at in enumerate((first, other)):
            many = BLOCK * (part + 1)
            score = dot(queries[pl.ds(at, BLOCK), base : base + 256], keys[head, :, :many])
            if part == 0:
                score = jnp.where(seen, score, -jnp.inf)
            else:
                score = jnp.concatenate([score[:, :BLOCK], jnp.where(seen, score[:, BLOCK:], -jnp.inf)], axis=1)
            top = jnp.max(score, axis=1, keepdims=True)
            weight = jnp.exp2((score - top) * GAIN).astype(BF16)
            got = dot(weight, value[:many])
            acc_out[pl.ds(at, BLOCK), columns] = got[:, :VAL]
            stat[part] = jnp.where(lane == head, got[:, VAL:], stat[part])
            stat[part] = jnp.where(lane == heads + head, top, stat[part])
    stat_out[pl.ds(first, BLOCK), :] = stat[0]
    stat_out[pl.ds(other, BLOCK), :] = stat[1]


def prior_kernel(ids, queries, near, far, w_near, w_more, w_far, key_up_t, value_up, acc_in, stat_in, out, lat, keys, values, tail):
    turn = lax.axis_size("seq") // 2
    crossing = lax.rem(lax.axis_index("seq"), turn) == 0
    spot = lax.axis_index("head")

    def positions():
        one = jnp.max(tail[ROPE : ROPE + 1, :128].astype(F32)).astype(jnp.int32)
        two = jnp.max(tail[ROPE : ROPE + 1, BLOCK : BLOCK + 128].astype(F32)).astype(jnp.int32)
        return one, two

    def from_chip_beside():
        tail[...] = near[NEAR * SHARD :, :]

    def from_other_half():
        tail[...] = w_near[SHARD:, :]

    pl.when(crossing)(from_other_half)
    pl.when(jnp.logical_not(crossing))(from_chip_beside)
    one, two = positions()
    first = pl.multiple_of(jnp.where(one < two, 0, BLOCK), BLOCK)
    low, high = jnp.minimum(one, two), jnp.maximum(one, two)
    pl.when(crossing)(lambda: place((w_near.at[:SHARD], *w_more, *w_far), spot ^ 7, first, lat))
    pl.when(jnp.logical_not(crossing))(lambda: place((near.at[: NEAR * SHARD], far), spot, first, lat))
    place_rope(tail.at[:ROPE], first, keys)
    project(lat, key_up_t, value_up, keys, values)
    heads = keys.shape[0]
    ones = jnp.ones((2 * BLOCK, VAL), BF16)

    def merged(part, many):
        def body():
            for head in range(heads):
                base = (head // 2) * 384 + (head % 2) * 128
                rows = pl.ds(part * BLOCK, BLOCK)
                columns = slice(head * VAL, (head + 1) * VAL)
                total = stat_in[rows, head : head + 1]
                if many == 0:
                    out[rows, columns] = (acc_in[rows, columns] / total).astype(BF16)
                    continue
                value = jnp.concatenate([values[:many, columns], ones[:many]], axis=1)
                score = dot(queries[rows, base : base + 256], keys[head, :, :many])
                before = stat_in[rows, heads + head : heads + head + 1]
                top = jnp.maximum(before, jnp.max(score, axis=1, keepdims=True))
                weight = jnp.exp2((score - top) * GAIN).astype(BF16)
                keep = jnp.exp2((before - top) * GAIN)
                got = dot(weight, value)
                total = got[:, VAL:] + total * keep
                out[rows, columns] = ((got[:, :VAL] + acc_in[rows, columns] * keep) / total).astype(BF16)

        return body

    for part in range(2):
        mine = ids[part]
        count = (low <= mine).astype(jnp.int32) + (high <= mine).astype(jnp.int32)
        for many in range(3):
            pl.when(count == many)(merged(part, many * BLOCK))


VMEM = pl.BlockSpec(memory_space=pltpu.VMEM)
SMEM = pl.BlockSpec(memory_space=pltpu.SMEM)


def scratch_of(tokens, heads, features):
    return [
        pltpu.VMEM((features, tokens), BF16),
        pltpu.VMEM((heads, 256, tokens), BF16),
        pltpu.VMEM((tokens, heads * VAL), BF16),
    ]


def own_part(ids, queries, pieces, rope, key_up_t, value_up):
    tokens, heads = queries.shape[0], value_up.shape[1] // VAL
    return pl.pallas_call(
        own_kernel,
        out_shape=(jax.ShapeDtypeStruct((tokens, heads * VAL), F32), jax.ShapeDtypeStruct((tokens, 128), F32)),
        in_specs=[SMEM] + [VMEM] * 8,
        out_specs=(VMEM, VMEM),
        scratch_shapes=scratch_of(tokens, heads, value_up.shape[0]),
        compiler_params=pltpu.CompilerParams(vmem_limit_bytes=40 << 20),
        cost_estimate=pl.CostEstimate(flops=3 << 30, bytes_accessed=8 << 20, transcendentals=1 << 21),
        name="own_part",
    )(ids, queries, *pieces, rope, key_up_t, value_up)


def prior_part(ids, queries, near, far, w_near, w_more, w_far, key_up_t, value_up, acc, stat):
    tokens, heads = queries.shape[0], value_up.shape[1] // VAL

    def kernel(ids, queries, near, far, w_near, wa, wb, wc, wd, we, *rest):
        prior_kernel(ids, queries, near, far, w_near, (wa, wb), (wc, wd, we), *rest)

    return pl.pallas_call(
        kernel,
        out_shape=jax.ShapeDtypeStruct((tokens, heads * VAL), BF16),
        in_specs=[SMEM] + [VMEM] * 13,
        out_specs=VMEM,
        scratch_shapes=scratch_of(tokens, heads, value_up.shape[0]) + [pltpu.VMEM((ROPE + ID_ROWS, tokens), BF16)],
        compiler_params=pltpu.CompilerParams(vmem_limit_bytes=40 << 20),
        cost_estimate=pl.CostEstimate(flops=4 << 30, bytes_accessed=8 << 20, transcendentals=1 << 21),
        name="prior_part",
    )(ids, queries, near, far, w_near, *w_more, *w_far, key_up_t, value_up, acc, stat)


def swapped(shard, by):
    return lax.ppermute(shard, "head", [(i, i ^ by) for i in range(lax.axis_size("head"))])


def joined(*parts):
    return jnp.concatenate(parts, axis=0)


def shards(queries, latent, key_rope, key_up, value_up, block_ids):
    groups, peers = lax.axis_size("seq"), lax.axis_size("head")
    turn = groups // 2
    both = ("seq", "head")
    tokens = queries.shape[0]

    def beside(shard):
        return lax.ppermute(shard, "seq", [(i, i + 1) for i in range(groups) if (i + 1) % turn])

    def across(shard, by):
        pairs = [(i, (i + 1) % groups) for i in range(turn - 1, groups, turn)]
        return lax.ppermute(shard, both, [(s * peers + (h ^ by), t * peers + h) for s, t in pairs for h in range(peers)])

    def swapped_there(shard, by):
        return lax.ppermute(shard, both, [(t * peers + (h ^ by), t * peers + h) for t in range(0, groups, turn) for h in range(peers)])

    mine, rope = latent.T, key_rope.T
    id_row = jnp.repeat(block_ids.astype(BF16), tokens // 2)
    tail = joined(rope, jnp.broadcast_to(id_row[None], (ID_ROWS, tokens)))
    by4, by2 = swapped(mine, 4), swapped(mine, 2)
    w_near = across(joined(mine, tail), 7)
    w_more = (across(mine, 3), across(mine, 5))
    held = joined(mine, by4, by2)
    got = (swapped(held, 1), swapped(by4, 2), swapped(by4, 3))
    near = beside(joined(held, tail))
    w_far = (swapped_there(joined(w_near[:SHARD], *w_more), 1), swapped_there(w_more[0], 2), swapped_there(w_more[0], 3))
    far = beside(joined(*got))
    key_up_t = key_up.T
    acc, stat = own_part(block_ids, queries, (held, *got), rope, key_up_t, value_up)
    return prior_part(block_ids, queries, near, far, w_near, w_more, w_far, key_up_t, value_up, acc, stat)


def solution(mesh):
    in_specs = (
        P("seq", "head"),
        P("seq", "head"),
        P("seq", None),
        P(None, "head"),
        P(None, "head"),
        P("seq"),
    )
    out_specs = P("seq", "head")
    return jax.shard_map(shards, mesh=mesh, in_specs=in_specs, out_specs=out_specs, check_vma=False)
```

```python
import math

import jax
import jax.numpy as jnp
from jax import lax
from jax.experimental import pallas as pl
from jax.experimental.pallas import tpu as pltpu
from jax.sharding import PartitionSpec as P

ROPE = 64
NOPE = 128
VAL = 128
BLOCK = 256
SHARD = 64
ID_ROWS = 16
GAIN = math.log2(math.e) / math.sqrt(NOPE + ROPE)
ORDER = (0, 4, 1, 5, 2, 6, 3, 7)
NEAR = 2
F32 = jnp.float32
BF16 = jnp.bfloat16


def dot(a, b):
    return jnp.dot(a, b, preferred_element_type=F32)


def place(pieces, at, first, lat):
    rows = [(piece, r) for piece in pieces for r in range(0, piece.shape[0], SHARD)]
    other = pl.multiple_of(BLOCK - first, BLOCK)
    for (piece, r), which in zip(rows, ORDER, strict=True):
        to = pl.ds(pl.multiple_of((at ^ which) * SHARD, SHARD), SHARD)
        lat[to, :BLOCK] = piece[r : r + SHARD, pl.ds(first, BLOCK)]
        lat[to, BLOCK:] = piece[r : r + SHARD, pl.ds(other, BLOCK)]


def place_rope(rope_in, first, keys):
    other = pl.multiple_of(BLOCK - first, BLOCK)
    rope = jnp.concatenate([rope_in[:, pl.ds(first, BLOCK)], rope_in[:, pl.ds(other, BLOCK)]], axis=1)
    none = jnp.zeros_like(rope)
    for head in range(keys.shape[0]):
        if head % 2 == 0:
            keys[head, NOPE : NOPE + ROPE, :] = rope
            keys[head, NOPE + ROPE :, :] = none
        else:
            keys[head, :ROPE, :] = none
            keys[head, ROPE + NOPE :, :] = rope


def project(lat, key_up_t, value_up, keys, values):
    features = lat[...]
    for pair in range(keys.shape[0] // 2):
        part = dot(key_up_t[pair * 256 : (pair + 1) * 256, :], features).astype(BF16)
        keys[2 * pair, :NOPE, :] = part[:NOPE]
        keys[2 * pair + 1, ROPE : ROPE + NOPE, :] = part[NOPE:]
    rows = features.T
    for pair in range(keys.shape[0] // 2):
        columns = slice(pair * 256, (pair + 1) * 256)
        values[:, columns] = dot(rows, value_up[:, columns]).astype(BF16)


def own_kernel(ids, queries, a, b, c, d, rope, key_up_t, value_up, acc_out, sum_out, top_out, lat, keys, values):
    first = pl.multiple_of(jnp.where(ids[0] < ids[1], 0, BLOCK), BLOCK)
    other = pl.multiple_of(BLOCK - first, BLOCK)
    place((a, b, c, d), lax.axis_index("head"), first, lat)
    place_rope(rope, first, keys)
    project(lat, key_up_t, value_up, keys, values)
    heads = keys.shape[0]
    row = lax.broadcasted_iota(jnp.int32, (BLOCK, BLOCK), 0)
    col = lax.broadcasted_iota(jnp.int32, (BLOCK, BLOCK), 1)
    seen = col <= row
    ones = jnp.ones((2 * BLOCK, VAL), BF16)
    def scores(head):
        base = (head // 2) * 384 + (head % 2) * 128
        return [dot(queries[pl.ds(at, BLOCK), base : base + 256], keys[head, :, : BLOCK * (part + 1)]) for part, at in enumerate((first, other))]

    ahead = scores(0)
    for head in range(heads):
        now = ahead
        if head + 1 < heads:
            ahead = scores(head + 1)
        columns = slice(head * VAL, (head + 1) * VAL)
        value = jnp.concatenate([values[:, columns], ones], axis=1)
        for part, at in enumerate((first, other)):
            many = BLOCK * (part + 1)
            score = now[part]
            if part == 0:
                score = jnp.where(seen, score, -jnp.inf)
            else:
                score = jnp.concatenate([score[:, :BLOCK], jnp.where(seen, score[:, BLOCK:], -jnp.inf)], axis=1)
            top = jnp.max(score, axis=1, keepdims=True)
            weight = jnp.exp2((score - top) * GAIN).astype(BF16)
            got = dot(weight, value[:many])
            acc_out[pl.ds(at, BLOCK), columns] = got[:, :VAL]
            sum_out[pl.ds(at, BLOCK), columns] = got[:, VAL:]
            top_out[pl.ds(at, BLOCK), columns] = jnp.broadcast_to(top, (BLOCK, VAL))


def prior_kernel(ids, queries, near, far, w_near, w_more, w_far, key_up_t, value_up, acc_in, sum_in, top_in, out, lat, keys, values, tail):
    turn = lax.axis_size("seq") // 2
    crossing = lax.rem(lax.axis_index("seq"), turn) == 0
    spot = lax.axis_index("head")

    def positions():
        one = jnp.max(tail[ROPE : ROPE + 1, :128].astype(F32)).astype(jnp.int32)
        two = jnp.max(tail[ROPE : ROPE + 1, BLOCK : BLOCK + 128].astype(F32)).astype(jnp.int32)
        return one, two

    def from_chip_beside():
        tail[...] = near[NEAR * SHARD :, :]

    def from_other_half():
        tail[...] = w_near[SHARD:, :]

    pl.when(crossing)(from_other_half)
    pl.when(jnp.logical_not(crossing))(from_chip_beside)
    one, two = positions()
    first = pl.multiple_of(jnp.where(one < two, 0, BLOCK), BLOCK)
    low, high = jnp.minimum(one, two), jnp.maximum(one, two)
    pl.when(crossing)(lambda: place((w_near.at[:SHARD], *w_more, *w_far), spot ^ 7, first, lat))
    pl.when(jnp.logical_not(crossing))(lambda: place((near.at[: NEAR * SHARD], far), spot, first, lat))
    place_rope(tail.at[:ROPE], first, keys)
    project(lat, key_up_t, value_up, keys, values)
    heads = keys.shape[0]
    ones = jnp.ones((2 * BLOCK, VAL), BF16)

    def merged(start, size, many):
        rows = slice(start, start + size)

        def scores(head):
            base = (head // 2) * 384 + (head % 2) * 128
            return dot(queries[rows, base : base + 256], keys[head, :, :many])

        def body():
            ahead = scores(0)
            for head in range(heads):
                score = ahead
                if head + 1 < heads:
                    ahead = scores(head + 1)
                columns = slice(head * VAL, (head + 1) * VAL)
                value = jnp.concatenate([values[:many, columns], ones[:many]], axis=1)
                before = top_in[rows, columns]
                top = jnp.maximum(before, jnp.max(score, axis=1, keepdims=True))
                weight = jnp.exp2((score - jnp.concatenate([top] * (many // VAL), axis=1)) * GAIN).astype(BF16)
                keep = jnp.exp2((before - top) * GAIN)
                got = dot(weight, value)
                total = got[:, VAL:] + sum_in[rows, columns] * keep
                out[rows, columns] = ((got[:, :VAL] + acc_in[rows, columns] * keep) / total).astype(BF16)

        return body

    def alone(start):
        rows = slice(start, start + BLOCK)
        return lambda: out.__setitem__((rows, slice(None)), (acc_in[rows, :] / sum_in[rows, :]).astype(BF16))

    counts = [(low <= ids[part]).astype(jnp.int32) + (high <= ids[part]).astype(jnp.int32) for part in range(2)]
    whole = jnp.logical_and(counts[0] == 2, counts[1] == 2)
    pl.when(whole)(merged(0, 2 * BLOCK, 2 * BLOCK))
    for part in range(2):
        start = part * BLOCK
        pl.when(counts[part] == 0)(alone(start))
        pl.when(counts[part] == 1)(merged(start, BLOCK, BLOCK))
        pl.when(jnp.logical_and(counts[part] == 2, jnp.logical_not(whole)))(merged(start, BLOCK, 2 * BLOCK))


VMEM = pl.BlockSpec(memory_space=pltpu.VMEM)
SMEM = pl.BlockSpec(memory_space=pltpu.SMEM)


def scratch_of(tokens, heads, features):
    return [
        pltpu.VMEM((features, tokens), BF16),
        pltpu.VMEM((heads, 256, tokens), BF16),
        pltpu.VMEM((tokens, heads * VAL), BF16),
    ]


def own_part(ids, queries, pieces, rope, key_up_t, value_up):
    tokens, heads = queries.shape[0], value_up.shape[1] // VAL
    return pl.pallas_call(
        own_kernel,
        out_shape=(jax.ShapeDtypeStruct((tokens, heads * VAL), F32),) * 3,
        in_specs=[SMEM] + [VMEM] * 8,
        out_specs=(VMEM,) * 3,
        scratch_shapes=scratch_of(tokens, heads, value_up.shape[0]),
        compiler_params=pltpu.CompilerParams(vmem_limit_bytes=20 << 20),
        cost_estimate=pl.CostEstimate(flops=3 << 30, bytes_accessed=8 << 20, transcendentals=1 << 21),
        name="own_part",
    )(ids, queries, *pieces, rope, key_up_t, value_up)


def prior_part(ids, queries, near, far, w_near, w_more, w_far, key_up_t, value_up, state):
    tokens, heads = queries.shape[0], value_up.shape[1] // VAL

    def kernel(ids, queries, near, far, w_near, wa, wb, wc, wd, *rest):
        prior_kernel(ids, queries, near, far, w_near, (wa,), (wb, wc, wd), *rest)

    return pl.pallas_call(
        kernel,
        out_shape=jax.ShapeDtypeStruct((tokens, heads * VAL), BF16),
        in_specs=[SMEM] + [VMEM] * 13,
        out_specs=VMEM,
        scratch_shapes=scratch_of(tokens, heads, value_up.shape[0]) + [pltpu.VMEM((ROPE + ID_ROWS, tokens), BF16)],
        compiler_params=pltpu.CompilerParams(vmem_limit_bytes=20 << 20),
        cost_estimate=pl.CostEstimate(flops=4 << 30, bytes_accessed=8 << 20, transcendentals=1 << 21),
        name="prior_part",
    )(ids, queries, near, far, w_near, *w_more, *w_far, key_up_t, value_up, *state)


def leaving_kernel(ids, mine, rope, out):
    first = SHARD + ROPE
    out[:SHARD, :] = mine[...]
    out[SHARD:first, :] = rope[...]
    slot = lax.broadcasted_iota(jnp.int32, (ID_ROWS, out.shape[1]), 1) // BLOCK
    out[first:, :] = jnp.where(slot == 0, ids[0], ids[1]).astype(F32).astype(BF16)


def leaving_part(ids, mine, rope):
    return pl.pallas_call(
        leaving_kernel,
        out_shape=jax.ShapeDtypeStruct((SHARD + ROPE + ID_ROWS, mine.shape[1]), BF16),
        in_specs=[SMEM, VMEM, VMEM],
        out_specs=VMEM,
        compiler_params=pltpu.CompilerParams(vmem_limit_bytes=4 << 20),
        name="leaving_part",
    )(ids, mine, rope)


def weights_kernel(key_up, value_up, key_out, value_out):
    key_out[...] = key_up[...].T
    value_out[...] = value_up[...]


def weights_part(key_up, value_up):
    return pl.pallas_call(
        weights_kernel,
        out_shape=(jax.ShapeDtypeStruct(key_up.shape[::-1], BF16), jax.ShapeDtypeStruct(value_up.shape, BF16)),
        in_specs=[VMEM, VMEM],
        out_specs=(VMEM, VMEM),
        compiler_params=pltpu.CompilerParams(vmem_limit_bytes=16 << 20),
        name="weights_part",
    )(key_up, value_up)


def swapped(shard, by):
    return lax.ppermute(shard, "head", [(i, i ^ by) for i in range(lax.axis_size("head"))])


def joined(*parts):
    return jnp.concatenate(parts, axis=0)


def shards(queries, latent, key_rope, key_up, value_up, block_ids):
    groups, peers = lax.axis_size("seq"), lax.axis_size("head")
    turn = groups // 2
    both = ("seq", "head")
    tokens = queries.shape[0]

    def beside(shard):
        return lax.ppermute(shard, "seq", [(i, i + 1) for i in range(groups) if (i + 1) % turn])

    def across(shard, by):
        pairs = [(i, (i + 1) % groups) for i in range(turn - 1, groups, turn)]
        return lax.ppermute(shard, both, [(s * peers + (h ^ by), t * peers + h) for s, t in pairs for h in range(peers)])

    def swapped_there(shard, by):
        return lax.ppermute(shard, both, [(t * peers + (h ^ by), t * peers + h) for t in range(0, groups, turn) for h in range(peers)])

    mine, rope = latent.T, key_rope.T
    by4 = swapped(mine, 4)
    leaving = leaving_part(block_ids, mine, rope)
    w_near, w_more = across(leaving, 7), (across(leaving, 3)[:SHARD],)
    key_up_t, value_up = weights_part(key_up, value_up)
    held = joined(leaving[:SHARD], by4)
    got = tuple(swapped(held, by) for by in (1, 2, 3))
    near = beside(joined(held, leaving[SHARD:]))
    w_held = joined(w_near[:SHARD], *w_more)
    w_far = tuple(swapped_there(w_held, by) for by in (1, 2, 3))
    far = beside(joined(*got))
    state = own_part(block_ids, queries, (held, *got), rope, key_up_t, value_up)
    return prior_part(block_ids, queries, near, far, w_near, w_more, w_far, key_up_t, value_up, state)


def solution(mesh):
    in_specs = (
        P("seq", "head"),
        P("seq", "head"),
        P("seq", None),
        P(None, "head"),
        P(None, "head"),
        P("seq"),
    )
    out_specs = P("seq", "head")
    return jax.shard_map(shards, mesh=mesh, in_specs=in_specs, out_specs=out_specs, check_vma=False)
```

```python
import math

import jax
import jax.numpy as jnp
from jax import lax
from jax.experimental import pallas as pl
from jax.experimental.pallas import tpu as pltpu
from jax.sharding import PartitionSpec as P

ROPE = 64
NOPE = 128
VAL = 128
BLOCK = 256
SHARD = 64
ID_ROWS = 16
GAIN = math.log2(math.e) / math.sqrt(NOPE + ROPE)
ORDER = (0, 4, 1, 5, 2, 6, 3, 7)
NEAR = 2
F32 = jnp.float32
BF16 = jnp.bfloat16


def dot(a, b):
    return jnp.dot(a, b, preferred_element_type=F32)


def place(pieces, at, first, lat):
    rows = [(piece, r) for piece in pieces for r in range(0, piece.shape[0], SHARD)]
    other = pl.multiple_of(BLOCK - first, BLOCK)
    for (piece, r), which in zip(rows, ORDER, strict=True):
        to = pl.ds(pl.multiple_of((at ^ which) * SHARD, SHARD), SHARD)
        lat[to, :BLOCK] = piece[r : r + SHARD, pl.ds(first, BLOCK)]
        lat[to, BLOCK:] = piece[r : r + SHARD, pl.ds(other, BLOCK)]


def place_rope(rope_in, first, keys):
    other = pl.multiple_of(BLOCK - first, BLOCK)
    rope = jnp.concatenate([rope_in[:, pl.ds(first, BLOCK)], rope_in[:, pl.ds(other, BLOCK)]], axis=1)
    none = jnp.zeros_like(rope)
    for head in range(keys.shape[0]):
        if head % 2 == 0:
            keys[head, NOPE : NOPE + ROPE, :] = rope
            keys[head, NOPE + ROPE :, :] = none
        else:
            keys[head, :ROPE, :] = none
            keys[head, ROPE + NOPE :, :] = rope


def project(lat, key_up_t, value_up, keys, values):
    features = lat[...]
    for pair in range(keys.shape[0] // 2):
        part = dot(key_up_t[pair * 256 : (pair + 1) * 256, :], features).astype(BF16)
        keys[2 * pair, :NOPE, :] = part[:NOPE]
        keys[2 * pair + 1, ROPE : ROPE + NOPE, :] = part[NOPE:]
    rows = features.T
    for pair in range(keys.shape[0] // 2):
        columns = slice(pair * 256, (pair + 1) * 256)
        values[:, columns] = dot(rows, value_up[:, columns]).astype(BF16)


def own_kernel(ids, queries, a, b, c, d, rope, key_up_t, value_up, acc_out, sum_out, top_out, lat, keys, values):
    first = pl.multiple_of(jnp.where(ids[0] < ids[1], 0, BLOCK), BLOCK)
    other = pl.multiple_of(BLOCK - first, BLOCK)
    place((a, b, c, d), lax.axis_index("head"), first, lat)
    place_rope(rope, first, keys)
    project(lat, key_up_t, value_up, keys, values)
    heads = keys.shape[0]
    row = lax.broadcasted_iota(jnp.int32, (BLOCK, BLOCK), 0)
    col = lax.broadcasted_iota(jnp.int32, (BLOCK, BLOCK), 1)
    seen = col <= row
    ones = jnp.ones((2 * BLOCK, VAL), BF16)
    def scores(head):
        base = (head // 2) * 384 + (head % 2) * 128
        return [dot(queries[pl.ds(at, BLOCK), base : base + 256], keys[head, :, : BLOCK * (part + 1)]) for part, at in enumerate((first, other))]

    ahead = scores(0)
    for head in range(heads):
        now = ahead
        if head + 1 < heads:
            ahead = scores(head + 1)
        columns = slice(head * VAL, (head + 1) * VAL)
        value = jnp.concatenate([values[:, columns], ones], axis=1)
        for part, at in enumerate((first, other)):
            many = BLOCK * (part + 1)
            score = now[part]
            if part == 0:
                score = jnp.where(seen, score, -jnp.inf)
            else:
                score = jnp.concatenate([score[:, :BLOCK], jnp.where(seen, score[:, BLOCK:], -jnp.inf)], axis=1)
            top = jnp.max(score, axis=1, keepdims=True)
            weight = jnp.exp2((score - top) * GAIN).astype(BF16)
            got = dot(weight, value[:many])
            acc_out[pl.ds(at, BLOCK), columns] = got[:, :VAL]
            sum_out[pl.ds(at, BLOCK), columns] = got[:, VAL:]
            top_out[pl.ds(at, BLOCK), columns] = jnp.broadcast_to(top, (BLOCK, VAL))


def prior_kernel(ids, queries, near, far, there, across, key_up_t, value_up, acc_in, sum_in, top_in, out, lat, keys, values, tail):
    turn = lax.axis_size("seq") // 2
    crossing = lax.rem(lax.axis_index("seq"), turn) == 0
    spot = lax.axis_index("head")

    def tail_from(source):
        def body():
            tail[...] = source[...]

        return body

    pl.when(crossing)(tail_from(there.at[SHARD:]))
    pl.when(jnp.logical_not(crossing))(tail_from(near.at[NEAR * SHARD :]))
    one = jnp.max(tail[ROPE : ROPE + 1, :128].astype(F32)).astype(jnp.int32)
    two = jnp.max(tail[ROPE : ROPE + 1, BLOCK : BLOCK + 128].astype(F32)).astype(jnp.int32)
    first = pl.multiple_of(jnp.where(one < two, 0, BLOCK), BLOCK)
    low, high = jnp.minimum(one, two), jnp.maximum(one, two)
    pl.when(crossing)(lambda: place(across, spot ^ 4, first, lat))
    pl.when(jnp.logical_not(crossing))(lambda: place((near.at[: NEAR * SHARD], far), spot, first, lat))
    place_rope(tail.at[:ROPE], first, keys)
    project(lat, key_up_t, value_up, keys, values)
    heads = keys.shape[0]
    ones = jnp.ones((2 * BLOCK, VAL), BF16)

    def merged(start, size, many):
        rows = slice(start, start + size)

        def scores(head):
            base = (head // 2) * 384 + (head % 2) * 128
            return dot(queries[rows, base : base + 256], keys[head, :, :many])

        def body():
            ahead = scores(0)
            for head in range(heads):
                score = ahead
                if head + 1 < heads:
                    ahead = scores(head + 1)
                columns = slice(head * VAL, (head + 1) * VAL)
                value = jnp.concatenate([values[:many, columns], ones[:many]], axis=1)
                before = top_in[rows, columns]
                top = jnp.maximum(before, jnp.max(score, axis=1, keepdims=True))
                weight = jnp.exp2((score - jnp.concatenate([top] * (many // VAL), axis=1)) * GAIN).astype(BF16)
                keep = jnp.exp2((before - top) * GAIN)
                got = dot(weight, value)
                total = got[:, VAL:] + sum_in[rows, columns] * keep
                out[rows, columns] = ((got[:, :VAL] + acc_in[rows, columns] * keep) / total).astype(BF16)

        return body

    def alone(start):
        rows = slice(start, start + BLOCK)
        return lambda: out.__setitem__((rows, slice(None)), (acc_in[rows, :] / sum_in[rows, :]).astype(BF16))

    counts = [(low <= ids[part]).astype(jnp.int32) + (high <= ids[part]).astype(jnp.int32) for part in range(2)]
    whole = jnp.logical_and(counts[0] == 2, counts[1] == 2)
    pl.when(whole)(merged(0, 2 * BLOCK, 2 * BLOCK))
    for part in range(2):
        start = part * BLOCK
        pl.when(counts[part] == 0)(alone(start))
        pl.when(counts[part] == 1)(merged(start, BLOCK, BLOCK))
        pl.when(jnp.logical_and(counts[part] == 2, jnp.logical_not(whole)))(merged(start, BLOCK, 2 * BLOCK))


VMEM = pl.BlockSpec(memory_space=pltpu.VMEM)
SMEM = pl.BlockSpec(memory_space=pltpu.SMEM)


def scratch_of(tokens, heads, features):
    return [
        pltpu.VMEM((features, tokens), BF16),
        pltpu.VMEM((heads, 256, tokens), BF16),
        pltpu.VMEM((tokens, heads * VAL), BF16),
    ]


def own_part(ids, queries, pieces, rope, key_up_t, value_up):
    tokens, heads = queries.shape[0], value_up.shape[1] // VAL
    return pl.pallas_call(
        own_kernel,
        out_shape=(jax.ShapeDtypeStruct((tokens, heads * VAL), F32),) * 3,
        in_specs=[SMEM] + [VMEM] * 8,
        out_specs=(VMEM,) * 3,
        scratch_shapes=scratch_of(tokens, heads, value_up.shape[0]),
        compiler_params=pltpu.CompilerParams(vmem_limit_bytes=20 << 20),
        cost_estimate=pl.CostEstimate(flops=3 << 30, bytes_accessed=8 << 20, transcendentals=1 << 21),
        name="own_part",
    )(ids, queries, *pieces, rope, key_up_t, value_up)


def prior_part(ids, queries, near, far, there, across, key_up_t, value_up, state):
    tokens, heads = queries.shape[0], value_up.shape[1] // VAL

    def kernel(ids, queries, near, far, there, wa, wb, wc, wd, *rest):
        prior_kernel(ids, queries, near, far, there, (wa, wb, wc, wd), *rest)

    return pl.pallas_call(
        kernel,
        out_shape=jax.ShapeDtypeStruct((tokens, heads * VAL), BF16),
        in_specs=[SMEM] + [VMEM] * 13,
        out_specs=VMEM,
        scratch_shapes=scratch_of(tokens, heads, value_up.shape[0]) + [pltpu.VMEM((ROPE + ID_ROWS, tokens), BF16)],
        compiler_params=pltpu.CompilerParams(vmem_limit_bytes=20 << 20),
        cost_estimate=pl.CostEstimate(flops=4 << 30, bytes_accessed=8 << 20, transcendentals=1 << 21),
        name="prior_part",
    )(ids, queries, near, far, there, *across, key_up_t, value_up, *state)


def leaving_kernel(ids, mine, rope, out):
    first = SHARD + ROPE
    out[:SHARD, :] = mine[...]
    out[SHARD:first, :] = rope[...]
    slot = lax.broadcasted_iota(jnp.int32, (ID_ROWS, out.shape[1]), 1) // BLOCK
    out[first:, :] = jnp.where(slot == 0, ids[0], ids[1]).astype(F32).astype(BF16)


def leaving_part(ids, mine, rope):
    return pl.pallas_call(
        leaving_kernel,
        out_shape=jax.ShapeDtypeStruct((SHARD + ROPE + ID_ROWS, mine.shape[1]), BF16),
        in_specs=[SMEM, VMEM, VMEM],
        out_specs=VMEM,
        compiler_params=pltpu.CompilerParams(vmem_limit_bytes=4 << 20),
        name="leaving_part",
    )(ids, mine, rope)


def weights_kernel(key_up, value_up, key_out, value_out):
    key_out[...] = key_up[...].T
    value_out[...] = value_up[...]


def weights_part(key_up, value_up):
    return pl.pallas_call(
        weights_kernel,
        out_shape=(jax.ShapeDtypeStruct(key_up.shape[::-1], BF16), jax.ShapeDtypeStruct(value_up.shape, BF16)),
        in_specs=[VMEM, VMEM],
        out_specs=(VMEM, VMEM),
        compiler_params=pltpu.CompilerParams(vmem_limit_bytes=16 << 20),
        name="weights_part",
    )(key_up, value_up)


def swapped(shard, by):
    return lax.ppermute(shard, "head", [(i, i ^ by) for i in range(lax.axis_size("head"))])


def joined(*parts):
    return jnp.concatenate(parts, axis=0)


def shards(queries, latent, key_rope, key_up, value_up, block_ids):
    groups, peers = lax.axis_size("seq"), lax.axis_size("head")
    turn = groups // 2
    both = ("seq", "head")
    tokens = queries.shape[0]

    steps = [(i, (i + 1) % groups) for i in range(groups)]
    beside = [(s, t) for s, t in steps if t % turn]
    crossing = [(s, t) for s, t in steps if t % turn == 0]
    within = [(t, t) for _, t in crossing]

    def onward(shard, pairs, by=0):
        sent = [(s * peers + (h ^ by), t * peers + h) for s, t in pairs for h in range(peers)]
        return lax.ppermute(shard, both, sent)

    mine, rope = latent.T, key_rope.T
    by4 = swapped(mine, 4)
    arrived = onward(mine, crossing, 4)
    leaving = leaving_part(block_ids, mine, rope)
    there = onward(leaving, crossing, 4)
    held = joined(leaving[:SHARD], by4)
    got = tuple(swapped(held, by) for by in (1, 2, 3))
    arrived, key_up, value_up = lax.optimization_barrier((arrived, key_up, value_up))
    key_up_t, value_up = weights_part(key_up, value_up)
    w_held = joined(arrived, onward(arrived, within, 4))
    near = onward(joined(held, leaving[SHARD:]), beside)
    far = onward(joined(*got), beside)
    state = own_part(block_ids, queries, (held, *got), rope, key_up_t, value_up)
    across = (w_held, *(onward(w_held, within, by) for by in (1, 2, 3)))
    return prior_part(block_ids, queries, near, far, there, across, key_up_t, value_up, state)


def solution(mesh):
    in_specs = (
        P("seq", "head"),
        P("seq", "head"),
        P("seq", None),
        P(None, "head"),
        P(None, "head"),
        P("seq"),
    )
    out_specs = P("seq", "head")
    return jax.shard_map(shards, mesh=mesh, in_specs=in_specs, out_specs=out_specs, check_vma=False)
```

```python
import math

import jax
import jax.numpy as jnp
from jax import lax
from jax.experimental import pallas as pl
from jax.experimental.pallas import tpu as pltpu
from jax.sharding import PartitionSpec as P

ROPE = 64
NOPE = 128
VAL = 128
BLOCK = 256
SHARD = 64
ID_ROWS = 16
GAIN = math.log2(math.e) / math.sqrt(NOPE + ROPE)
ORDER = (0, 4, 1, 5, 2, 6, 3, 7)
NEAR = 2
F32 = jnp.float32
BF16 = jnp.bfloat16


def dot(a, b):
    return jnp.dot(a, b, preferred_element_type=F32)


def place(pieces, at, first, lat):
    rows = [(piece, r) for piece in pieces for r in range(0, piece.shape[0], SHARD)]
    if first is None:
        for (piece, r), which in zip(rows, ORDER, strict=True):
            lat[pl.ds(pl.multiple_of((at ^ which) * SHARD, SHARD), SHARD), :] = piece[r : r + SHARD, :]
        return
    other = pl.multiple_of(BLOCK - first, BLOCK)
    for (piece, r), which in zip(rows, ORDER, strict=True):
        to = pl.ds(pl.multiple_of((at ^ which) * SHARD, SHARD), SHARD)
        lat[to, :BLOCK] = piece[r : r + SHARD, pl.ds(first, BLOCK)]
        lat[to, BLOCK:] = piece[r : r + SHARD, pl.ds(other, BLOCK)]


def place_rope(rope_in, first, keys):
    if first is None:
        rope = rope_in[...]
    else:
        other = pl.multiple_of(BLOCK - first, BLOCK)
        rope = jnp.concatenate([rope_in[:, pl.ds(first, BLOCK)], rope_in[:, pl.ds(other, BLOCK)]], axis=1)
    none = jnp.zeros_like(rope)
    for head in range(keys.shape[0]):
        if head % 2 == 0:
            keys[head, NOPE : NOPE + ROPE, :] = rope
            keys[head, NOPE + ROPE :, :] = none
        else:
            keys[head, :ROPE, :] = none
            keys[head, ROPE + NOPE :, :] = rope


def project(lat, key_up_t, value_up, keys, values):
    features = lat[...]
    for pair in range(keys.shape[0] // 2):
        part = dot(key_up_t[pair * 256 : (pair + 1) * 256, :], features).astype(BF16)
        keys[2 * pair, :NOPE, :] = part[:NOPE]
        keys[2 * pair + 1, ROPE : ROPE + NOPE, :] = part[NOPE:]
    rows = features.T
    for pair in range(keys.shape[0] // 2):
        columns = slice(pair * 256, (pair + 1) * 256)
        values[:, columns] = dot(rows, value_up[:, columns]).astype(BF16)


def own_kernel(ids, queries, a, b, c, d, rope, key_up_t, value_up, acc_out, sum_out, top_out, lat, keys, values):
    first = pl.multiple_of(jnp.where(ids[0] < ids[1], 0, BLOCK), BLOCK)
    other = pl.multiple_of(BLOCK - first, BLOCK)
    place((a, b, c, d), lax.axis_index("head"), first, lat)
    place_rope(rope, first, keys)
    project(lat, key_up_t, value_up, keys, values)
    heads = keys.shape[0]
    row = lax.broadcasted_iota(jnp.int32, (BLOCK, BLOCK), 0)
    col = lax.broadcasted_iota(jnp.int32, (BLOCK, BLOCK), 1)
    seen = col <= row
    ones = jnp.ones((2 * BLOCK, VAL), BF16)
    def scores(head):
        base = (head // 2) * 384 + (head % 2) * 128
        return [dot(queries[pl.ds(at, BLOCK), base : base + 256], keys[head, :, : BLOCK * (part + 1)]) for part, at in enumerate((first, other))]

    ahead = scores(0)
    for head in range(heads):
        now = ahead
        if head + 1 < heads:
            ahead = scores(head + 1)
        columns = slice(head * VAL, (head + 1) * VAL)
        value = jnp.concatenate([values[:, columns], ones], axis=1)
        for part, at in enumerate((first, other)):
            many = BLOCK * (part + 1)
            score = now[part]
            if part == 0:
                score = jnp.where(seen, score, -jnp.inf)
            else:
                score = jnp.concatenate([score[:, :BLOCK], jnp.where(seen, score[:, BLOCK:], -jnp.inf)], axis=1)
            top = jnp.max(score, axis=1, keepdims=True)
            weight = jnp.exp2((score - top) * GAIN).astype(BF16)
            got = dot(weight, value[:many])
            acc_out[pl.ds(at, BLOCK), columns] = got[:, :VAL]
            sum_out[pl.ds(at, BLOCK), columns] = got[:, VAL:]
            top_out[pl.ds(at, BLOCK), columns] = jnp.broadcast_to(top, (BLOCK, VAL))


def prior_kernel(ids, queries, near, far, there, across, key_up_t, value_up, acc_in, sum_in, top_in, out, lat, keys, values, tail, done, sent):
    turn = lax.axis_size("seq") // 2
    crossing = lax.rem(lax.axis_index("seq"), turn) == 0
    spot = lax.axis_index("head")

    def tail_from(source):
        def body():
            tail[...] = source[...]

        return body

    pl.when(crossing)(tail_from(there.at[SHARD:]))
    pl.when(jnp.logical_not(crossing))(tail_from(near.at[NEAR * SHARD :]))
    pl.when(crossing)(lambda: place(across, spot ^ 4, None, lat))
    pl.when(jnp.logical_not(crossing))(lambda: place((near.at[: NEAR * SHARD], far), spot, None, lat))
    place_rope(tail.at[:ROPE], None, keys)
    project(lat, key_up_t, value_up, keys, values)
    one = jnp.max(tail[ROPE : ROPE + 1, :128].astype(F32)).astype(jnp.int32)
    two = jnp.max(tail[ROPE : ROPE + 1, BLOCK : BLOCK + 128].astype(F32)).astype(jnp.int32)
    first = pl.multiple_of(jnp.where(one < two, 0, BLOCK), BLOCK)
    low, high = jnp.minimum(one, two), jnp.maximum(one, two)
    heads = keys.shape[0]
    ones = jnp.ones((2 * BLOCK, VAL), BF16)

    def leave(rows, half):
        columns = slice(half * heads // 2 * VAL, (half + 1) * heads // 2 * VAL)
        return pltpu.make_async_copy(done.at[rows, columns], out.at[rows, columns], sent.at[half])

    def merged(start, size, many):
        rows = slice(start, start + size)
        seen = pl.ds(first if many == BLOCK else 0, many)

        def scores(head):
            base = (head // 2) * 384 + (head % 2) * 128
            return dot(queries[rows, base : base + 256], keys[head, :, seen])

        def body():
            ahead = scores(0)
            for head in range(heads):
                score = ahead
                if head + 1 < heads:
                    ahead = scores(head + 1)
                columns = slice(head * VAL, (head + 1) * VAL)
                value = jnp.concatenate([values[seen, columns], ones[:many]], axis=1)
                before = top_in[rows, columns]
                top = jnp.maximum(before, jnp.max(score, axis=1, keepdims=True))
                weight = jnp.exp2((score - jnp.concatenate([top] * (many // VAL), axis=1)) * GAIN).astype(BF16)
                keep = jnp.exp2((before - top) * GAIN)
                got = dot(weight, value)
                total = got[:, VAL:] + sum_in[rows, columns] * keep
                done[rows, columns] = ((got[:, :VAL] + acc_in[rows, columns] * keep) / total).astype(BF16)
                if head == heads // 2 - 1:
                    leave(rows, 0).start()
            leave(rows, 1).start()
            leave(rows, 0).wait()
            leave(rows, 1).wait()

        return body

    def alone(start):
        rows = slice(start, start + BLOCK)

        def body():
            done[rows, :] = (acc_in[rows, :] / sum_in[rows, :]).astype(BF16)
            for half in range(2):
                leave(rows, half).start()
            for half in range(2):
                leave(rows, half).wait()

        return body

    counts = [(low <= ids[part]).astype(jnp.int32) + (high <= ids[part]).astype(jnp.int32) for part in range(2)]
    whole = jnp.logical_and(counts[0] == 2, counts[1] == 2)
    pl.when(whole)(merged(0, 2 * BLOCK, 2 * BLOCK))
    for part in range(2):
        start = part * BLOCK
        pl.when(counts[part] == 0)(alone(start))
        pl.when(counts[part] == 1)(merged(start, BLOCK, BLOCK))
        pl.when(jnp.logical_and(counts[part] == 2, jnp.logical_not(whole)))(merged(start, BLOCK, 2 * BLOCK))


VMEM = pl.BlockSpec(memory_space=pltpu.VMEM)
SMEM = pl.BlockSpec(memory_space=pltpu.SMEM)


def scratch_of(tokens, heads, features):
    return [
        pltpu.VMEM((features, tokens), BF16),
        pltpu.VMEM((heads, 256, tokens), BF16),
        pltpu.VMEM((tokens, heads * VAL), BF16),
    ]


def own_part(ids, queries, pieces, rope, key_up_t, value_up):
    tokens, heads = queries.shape[0], value_up.shape[1] // VAL
    return pl.pallas_call(
        own_kernel,
        out_shape=(jax.ShapeDtypeStruct((tokens, heads * VAL), F32),) * 3,
        in_specs=[SMEM] + [VMEM] * 8,
        out_specs=(VMEM,) * 3,
        scratch_shapes=scratch_of(tokens, heads, value_up.shape[0]),
        compiler_params=pltpu.CompilerParams(vmem_limit_bytes=20 << 20),
        cost_estimate=pl.CostEstimate(flops=3 << 30, bytes_accessed=8 << 20, transcendentals=1 << 21),
        name="own_part",
    )(ids, queries, *pieces, rope, key_up_t, value_up)


def prior_part(ids, queries, near, far, there, across, key_up_t, value_up, state):
    tokens, heads = queries.shape[0], value_up.shape[1] // VAL

    def kernel(ids, queries, near, far, there, wa, wb, wc, wd, *rest):
        prior_kernel(ids, queries, near, far, there, (wa, wb, wc, wd), *rest)

    return pl.pallas_call(
        kernel,
        out_shape=jax.ShapeDtypeStruct((tokens, heads * VAL), BF16),
        in_specs=[SMEM] + [VMEM] * 13,
        out_specs=pl.BlockSpec(memory_space=pl.ANY),
        scratch_shapes=scratch_of(tokens, heads, value_up.shape[0]) + [
            pltpu.VMEM((ROPE + ID_ROWS, tokens), BF16),
            pltpu.VMEM((tokens, heads * VAL), BF16),
            pltpu.SemaphoreType.DMA((2,)),
        ],
        compiler_params=pltpu.CompilerParams(vmem_limit_bytes=20 << 20),
        cost_estimate=pl.CostEstimate(flops=4 << 30, bytes_accessed=8 << 20, transcendentals=1 << 21),
        name="prior_part",
    )(ids, queries, near, far, there, *across, key_up_t, value_up, *state)


def leaving_kernel(ids, mine, rope, out):
    first = SHARD + ROPE
    out[:SHARD, :] = mine[...]
    out[SHARD:first, :] = rope[...]
    slot = lax.broadcasted_iota(jnp.int32, (ID_ROWS, out.shape[1]), 1) // BLOCK
    out[first:, :] = jnp.where(slot == 0, ids[0], ids[1]).astype(F32).astype(BF16)


def leaving_part(ids, mine, rope):
    return pl.pallas_call(
        leaving_kernel,
        out_shape=jax.ShapeDtypeStruct((SHARD + ROPE + ID_ROWS, mine.shape[1]), BF16),
        in_specs=[SMEM, VMEM, VMEM],
        out_specs=VMEM,
        compiler_params=pltpu.CompilerParams(vmem_limit_bytes=4 << 20),
        name="leaving_part",
    )(ids, mine, rope)


def weights_kernel(key_up, value_up, key_out, value_out):
    key_out[...] = key_up[...].T
    value_out[...] = value_up[...]


def weights_part(key_up, value_up):
    return pl.pallas_call(
        weights_kernel,
        out_shape=(jax.ShapeDtypeStruct(key_up.shape[::-1], BF16), jax.ShapeDtypeStruct(value_up.shape, BF16)),
        in_specs=[VMEM, VMEM],
        out_specs=(VMEM, VMEM),
        compiler_params=pltpu.CompilerParams(vmem_limit_bytes=16 << 20),
        name="weights_part",
    )(key_up, value_up)


def swapped(shard, by):
    return lax.ppermute(shard, "head", [(i, i ^ by) for i in range(lax.axis_size("head"))])


def joined(*parts):
    return jnp.concatenate(parts, axis=0)


def shards(queries, latent, key_rope, key_up, value_up, block_ids):
    groups, peers = lax.axis_size("seq"), lax.axis_size("head")
    turn = groups // 2
    both = ("seq", "head")
    tokens = queries.shape[0]

    steps = [(i, (i + 1) % groups) for i in range(groups)]
    beside = [(s, t) for s, t in steps if t % turn]
    crossing = [(s, t) for s, t in steps if t % turn == 0]
    within = [(t, t) for _, t in crossing]

    def onward(shard, pairs, by=0):
        sent = [(s * peers + (h ^ by), t * peers + h) for s, t in pairs for h in range(peers)]
        return lax.ppermute(shard, both, sent)

    mine, rope = latent.T, key_rope.T
    by4 = swapped(mine, 4)
    arrived = onward(mine, crossing, 4)
    leaving = leaving_part(block_ids, mine, rope)
    there = onward(leaving, crossing, 4)
    held = joined(leaving[:SHARD], by4)
    got = tuple(swapped(held, by) for by in (1, 2, 3))
    arrived, key_up, value_up = lax.optimization_barrier((arrived, key_up, value_up))
    key_up_t, value_up = weights_part(key_up, value_up)
    w_held = joined(arrived, onward(arrived, within, 4))
    near = onward(joined(held, leaving[SHARD:]), beside)
    far = onward(joined(*got), beside)
    state = own_part(block_ids, queries, (held, *got), rope, key_up_t, value_up)
    across = (w_held, *(onward(w_held, within, by) for by in (1, 2, 3)))
    return prior_part(block_ids, queries, near, far, there, across, key_up_t, value_up, state)


def solution(mesh):
    in_specs = (
        P("seq", "head"),
        P("seq", "head"),
        P("seq", None),
        P(None, "head"),
        P(None, "head"),
        P("seq"),
    )
    out_specs = P("seq", "head")
    return jax.shard_map(shards, mesh=mesh, in_specs=in_specs, out_specs=out_specs, check_vma=False)
```
